512 devices in a mesh: contrast: 16 (over z, x_lo), dp: 32 (over x_hi, y, core).
Axes of the slice: x: 4 (x_hi: 2, x_lo: 2; x = x_hi * 2 + x_lo), y: 8, z: 8, core: 2. Of those that a mesh axis runs over, the one named last changes fastest.
Arguments:
- image_emb: bfloat16 [262144, 1152], P(('dp', 'contrast')), parts along dimension 0, may hold values from -0.17675781 to 0.17675781
- text_emb: bfloat16 [262144, 1152], P(('dp', 'contrast')), parts along dimension 0, may hold values from -0.17675781 to 0.17675781
- logit_scale: float32 [1], replicated, may hold values from 4 to 16
- logit_bias: float32 [1], replicated, may hold values from -3 to -1
Outputs:
- row_loss: float32 [262144], P(('dp', 'contrast')), parts along dimension 0
- grad_image: bfloat16 [262144, 1152], P(('dp', 'contrast')), parts along dimension 0
- grad_text: bfloat16 [262144, 1152], P(('dp', 'contrast')), parts along dimension 0
The draws below stay inside these ranges and needn't reach their ends.
There are 32 independent parts, one for each index of `dp`. The reference program is written for one: setup_inputs(seed, part) draws one part's arguments, and reference() takes and returns one part's arrays. A program takes and returns all parts, laid end to end along the dimension named above; an argument that names none is the same for every part. Nothing has to cross between parts.
All inputs are finite; a program needn't handle non-finite values.
Results may differ from the reference program's by a relative error of at most 0.006.
Values may be sent and summed in bfloat16 or wider, within the bound.
A program may use at most 64 MiB of HBM per device.

```python
import math
import jax
import jax.numpy as jnp
from jax import lax

D = 1152
ROWS_DEV = 512
TOKENS = 8192
N_CONTRAST = 16


def levels(stream_key, extent, pieces, smallest, largest):
    level, own = 1.0, jax.random.fold_in(stream_key, 6)
    for position, parts in pieces:
        heights = jnp.exp(jax.random.uniform(jax.random.fold_in(own, position), (parts,), jnp.float32, smallest / len(pieces), largest / len(pieces)))
        level = level * jnp.repeat(heights, extent[position] // parts).reshape([-1 if axis == position else 1 for axis in range(len(extent))])
    return level


def noise(key, shape, scale, most, shards=(), held_as=jnp.bfloat16):
    entries = scale * jax.random.normal(key, shape, jnp.float32)
    if shards:
        entries = entries * levels(key, shape, shards, -0.22, 0.18)
    return jnp.clip(entries, -most, most).astype(held_as)


def setup_inputs(seed: int = 0, part: int = 0) -> dict:
    seeds = jax.random.split(jax.random.key(seed), 5)
    part_keys = jax.random.split(jax.random.fold_in(seeds[4], part), 5)
    image_emb = noise(part_keys[0], (TOKENS, D), (D ** -0.5), 0.17675781, ((0, 16),))
    text_emb = noise(part_keys[1], (TOKENS, D), (D ** -0.5), 0.17675781, ((0, 16),))
    logit_scale = jnp.clip(jnp.exp(jax.random.uniform(seeds[2], (1,), jnp.float32, math.log(4.0), math.log(16.0))), 4.0, 16.0)
    logit_bias = jnp.clip(jax.random.uniform(seeds[3], (1,), jnp.float32, -3.0, -1.0), -3.0, -1.0)
    return {"image_emb": image_emb, "text_emb": text_emb, "logit_scale": logit_scale, "logit_bias": logit_bias}


def normalize(emb):
    full = emb.astype(jnp.float32)
    inv = lax.rsqrt(lax.optimization_barrier(jnp.sum(full * full, axis=1, keepdims=True)) + 1e-06)
    unit = full * inv
    return (unit, inv, unit.astype(jnp.bfloat16))

def pair_terms(xn, yn, scale, bias, diagonal):
    raw = lax.dot_general(xn, yn, (((1,), (1,)), ((), ())), preferred_element_type=jnp.float32)
    score = scale * raw + bias
    if diagonal:
        sign = jnp.where(jnp.eye(xn.shape[0], dtype=jnp.bool_), 1.0, -1.0).astype(jnp.float32)
    else:
        sign = -jnp.ones_like(score)
    loss = lax.optimization_barrier(jnp.sum(jax.nn.softplus(-sign * score), axis=1))
    slope = (-sign * jax.nn.sigmoid(-sign * score)).astype(jnp.bfloat16)
    grad_x = scale * jnp.dot(slope, yn, preferred_element_type=jnp.float32)
    grad_y = scale * lax.dot_general(slope, xn, (((0,), (0,)), ((), ())), preferred_element_type=jnp.float32)
    return (loss, grad_x, grad_y)

def finish(unit, inv, grad):
    return ((grad - unit * lax.optimization_barrier(jnp.sum(unit * grad, axis=1, keepdims=True))) * inv).astype(jnp.bfloat16)

def reference(image_emb, text_emb, logit_scale, logit_bias):
    scale = logit_scale[0]
    bias = logit_bias[0]
    unit_x, inv_x, xn = normalize(image_emb)
    unit_y, inv_y, yn = normalize(text_emb)
    rows = ROWS_DEV
    count = N_CONTRAST
    losses = []
    grad_x = jnp.zeros(unit_x.shape, jnp.float32)
    grad_y = jnp.zeros(unit_y.shape, jnp.float32)
    for block in range(count):
        xb = xn[block * rows:(block + 1) * rows]
        total = jnp.zeros((rows,), jnp.float32)
        for partner in [block, block ^ count // 2, block ^ 1]:
            yb = yn[partner * rows:(partner + 1) * rows]
            loss, gx, gy = pair_terms(xb, yb, scale, bias, partner == block)
            total = total + loss
            grad_x = grad_x.at[block * rows:(block + 1) * rows].add(gx)
            grad_y = grad_y.at[partner * rows:(partner + 1) * rows].add(gy)
        losses.append(total / (3.0 * rows))
    row_loss = jnp.concatenate(losses)
    return (row_loss, finish(unit_x, inv_x, grad_x), finish(unit_y, inv_y, grad_y))
```

```python
import functools

import jax
import jax.numpy as jnp
from jax import lax
from jax.experimental import pallas as pl
from jax.experimental.pallas import tpu as pltpu
from jax.sharding import PartitionSpec as P

MESH = pl.DeviceIdType.MESH
PIECE = 64
CHUNK = 128
FINISH = 64


def kernel(
    n,
    scale_ref,
    bias_ref,
    x_hbm,
    y_hbm,
    loss_out,
    gx_out,
    gy_out,
    raw,
    own,
    far,
    near,
    acc,
    inv,
    loss,
    load_sem,
    far_send,
    far_recv,
    near_send,
    near_recv,
    out_sem,
):
    rows, width = x_hbm.shape
    pieces = rows // PIECE
    me = lax.axis_index("contrast")
    far_id = {"contrast": lax.rem(me + n // 2, n)}
    near_id = {"contrast": me + 1 - 2 * lax.rem(me, 2)}
    scale = scale_ref[0]
    bias = bias_ref[0]

    barrier = pltpu.get_barrier_semaphore()
    for partner in (far_id, near_id):
        pl.semaphore_signal(barrier, inc=1, device_id=partner, device_id_type=MESH)

    def load(side, piece):
        source = (y_hbm, x_hbm)[side]
        return pltpu.make_async_copy(
            source.at[pl.ds(pl.multiple_of(piece * PIECE, PIECE), PIECE)],
            raw.at[pl.ds(pl.multiple_of(side * rows + piece * PIECE, PIECE), PIECE)],
            load_sem.at[side * pieces + piece],
        )

    def remote(target, buffer, send_sem, recv_sem, piece):
        at = pl.ds(pl.multiple_of(piece * PIECE, PIECE), PIECE)
        return pltpu.make_async_remote_copy(
            src_ref=own.at[at],
            dst_ref=buffer.at[at],
            send_sem=send_sem.at[piece],
            recv_sem=recv_sem.at[piece],
            device_id=target,
            device_id_type=MESH,
        )

    to_far = functools.partial(remote, far_id, far, far_send, far_recv)
    to_near = functools.partial(remote, near_id, near, near_send, near_recv)

    for side in (0, 1):
        @pl.loop(0, pieces)
        def _(piece):
            load(side, piece).start()

    for side in (0, 1):
        @pl.loop(0, pieces)
        def _(piece):
            load(side, piece).wait()
            at = pl.ds(pl.multiple_of(side * rows + piece * PIECE, PIECE), PIECE)
            full = raw[at, :].astype(jnp.float32)
            scaled = lax.rsqrt(jnp.sum(full * full, axis=1, keepdims=True) + 1e-06)
            inv[at, :] = scaled
            own[at, :] = (full * scaled).astype(jnp.bfloat16)
            if side == 0:
                @pl.when(piece == 0)
                def _():
                    pl.semaphore_wait(barrier, 2)
            to_far(side * pieces + piece).start()
            to_near(side * pieces + piece).start()

    acc[...] = jnp.zeros_like(acc)
    loss[...] = jnp.zeros_like(loss)

    def products(side, source, step, diagonal=False):
        other = (1 - side) * rows
        at = pl.ds(pl.multiple_of(side * rows + step * CHUNK, CHUNK), CHUNK)
        block = source[at, :]
        product = lax.dot_general(
            own[other:other + rows, :], block, (((1,), (1,)), ((), ())), preferred_element_type=jnp.float32
        )
        value = scale * product + bias
        if diagonal:
            row = lax.broadcasted_iota(jnp.int32, value.shape, 0)
            column = lax.broadcasted_iota(jnp.int32, value.shape, 1) + step * CHUNK
            matched = row == column
            value = jnp.where(matched, -value, value)
        small = jnp.exp(-jnp.abs(value))
        slope = jnp.where(value >= 0, 1.0, small) / (1.0 + small)
        if side == 0:
            loss[...] += jnp.maximum(value, 0.0) + jnp.log1p(small)
        if diagonal:
            slope = jnp.where(matched, -slope, slope)
        slope = slope.astype(jnp.bfloat16)
        mine = pl.ds(side * rows, rows)
        for start in range(0, width, 384):
            columns = slice(start, min(start + 384, width))
            acc[mine, columns] += jnp.dot(slope, block[:, columns], preferred_element_type=jnp.float32)

    for side in (0, 1):
        @pl.loop(0, rows // CHUNK)
        def _(step):
            products(side, own, step, diagonal=True)

    def finish(side, target):
        def out(step):
            at = pl.ds(pl.multiple_of(step * FINISH, FINISH), FINISH)
            here = pl.ds(pl.multiple_of((1 - side) * rows + step * FINISH, FINISH), FINISH)
            return here, pltpu.make_async_copy(raw.at[here], target.at[at], out_sem.at[side * (rows // FINISH) + step])

        @pl.loop(0, rows // FINISH)
        def _(step):
            here, copy = out(step)
            grad = scale * acc[pl.ds(pl.multiple_of(side * rows + step * FINISH, FINISH), FINISH), :]
            scaled = inv[here, :]
            unit = raw[here, :].astype(jnp.float32) * scaled
            along = jnp.sum(unit * grad, axis=1, keepdims=True)
            raw[here, :] = ((grad - unit * along) * scaled).astype(jnp.bfloat16)
            copy.start()

        return out

    per = CHUNK // PIECE
    outs = []
    for side, target in ((0, gx_out), (1, gy_out)):
        @pl.loop(0, rows // CHUNK)
        def _(step):
            for part in range(per):
                to_near(side * pieces + step * per + part).wait_recv()
            products(side, near, step)
            for part in range(per):
                to_far(side * pieces + step * per + part).wait_recv()
            products(side, far, step)

        if side == 0:
            loss_out[...] = jnp.sum(loss[...].T, axis=0) / (3.0 * rows)
        outs.append(finish(side, target))

    for out in outs:
        @pl.loop(0, rows // FINISH)
        def _(step):
            out(step)[1].wait()

    @pl.loop(0, 2 * pieces)
    def _(piece):
        to_far(piece).wait_send()
        to_near(piece).wait_send()


def local(image_emb, text_emb, logit_scale, logit_bias):
    rows, width = image_emb.shape
    n = lax.axis_size("contrast")
    copies = 2 * rows // PIECE
    both = pltpu.VMEM((2 * rows, width), jnp.bfloat16)
    dma = pltpu.SemaphoreType.DMA
    return pl.pallas_call(
        functools.partial(kernel, n),
        out_shape=(
            jax.ShapeDtypeStruct((rows,), jnp.float32),
            jax.ShapeDtypeStruct((rows, width), jnp.bfloat16),
            jax.ShapeDtypeStruct((rows, width), jnp.bfloat16),
        ),
        in_specs=[
            pl.BlockSpec(memory_space=pltpu.SMEM),
            pl.BlockSpec(memory_space=pltpu.SMEM),
            pl.BlockSpec(memory_space=pl.ANY),
            pl.BlockSpec(memory_space=pl.ANY),
        ],
        out_specs=(
            pl.BlockSpec(memory_space=pltpu.VMEM),
            pl.BlockSpec(memory_space=pl.ANY),
            pl.BlockSpec(memory_space=pl.ANY),
        ),
        scratch_shapes=[
            both,
            both,
            both,
            both,
            pltpu.VMEM((2 * rows, width), jnp.float32),
            pltpu.VMEM((2 * rows, 1), jnp.float32),
            pltpu.VMEM((rows, CHUNK), jnp.float32),
            dma((copies,)),
            dma((copies,)),
            dma((copies,)),
            dma((copies,)),
            dma((copies,)),
            dma((2 * rows // FINISH,)),
        ],
        compiler_params=pltpu.CompilerParams(
            collective_id=0, has_side_effects=True, vmem_limit_bytes=40 * 2**20
        ),
        cost_estimate=pl.CostEstimate(
            flops=24 * rows * rows * width, bytes_accessed=8 * rows * width, transcendentals=18 * rows * rows
        ),
        name="contrast",
    )(logit_scale, logit_bias, image_emb, text_emb)


def solution(mesh):
    placed = (P(("dp", "contrast"), None), P(("dp", "contrast"), None), P(), P())
    return jax.shard_map(
        local,
        mesh=mesh,
        in_specs=placed,
        out_specs=(P(("dp", "contrast")), P(("dp", "contrast"), None), P(("dp", "contrast"), None)),
        check_vma=False,
    )
```

```python
import functools

import jax
import jax.numpy as jnp
from jax import lax
from jax.experimental import pallas as pl
from jax.experimental.pallas import tpu as pltpu
from jax.sharding import PartitionSpec as P

MESH = pl.DeviceIdType.MESH
PIECE = 64
CHUNK = 128
FINISH = 64


def block(index, size, base=0):
    return pl.ds(pl.multiple_of(base + index * size, size), size)


def exchange(
    n,
    scale_hbm,
    bias_hbm,
    image_hbm,
    text_hbm,
    loss_out,
    image_grad,
    text_acc,
    text,
    text_inv,
    text_factor,
    image,
    image_inv,
    image_acc,
    own,
    far,
    near,
    loss,
    scale_ref,
    bias_ref,
    scalar_sem,
    load_sem,
    far_send,
    far_recv,
    near_send,
    near_recv,
):
    rows, width = image_hbm.shape
    pieces = rows // PIECE
    me = lax.axis_index("contrast")
    far_id = {"contrast": lax.rem(me + n // 2, n)}
    near_id = {"contrast": me + 1 - 2 * lax.rem(me, 2)}

    barrier = pltpu.get_barrier_semaphore()
    for partner in (far_id, near_id):
        pl.semaphore_signal(barrier, inc=1, device_id=partner, device_id_type=MESH)

    given = (text_hbm, image_hbm)
    held = (text, image)
    inverse = (text_inv, image_inv)
    total = (image_acc, text_acc)

    def load(side, piece):
        at = block(piece, PIECE)
        return pltpu.make_async_copy(given[side].at[at], held[side].at[at], load_sem.at[side * pieces + piece])

    def remote(target, buffer, send_sem, recv_sem, piece):
        at = block(piece, PIECE)
        return pltpu.make_async_remote_copy(
            src_ref=own.at[at],
            dst_ref=buffer.at[at],
            send_sem=send_sem.at[piece],
            recv_sem=recv_sem.at[piece],
            device_id=target,
            device_id_type=MESH,
        )

    to_far = functools.partial(remote, far_id, far, far_send, far_recv)
    to_near = functools.partial(remote, near_id, near, near_send, near_recv)

    load(0, 0).start()
    scalars = [
        pltpu.make_async_copy(source, target, scalar_sem.at[i])
        for i, (source, target) in enumerate(((scale_hbm, scale_ref), (bias_hbm, bias_ref)))
    ]
    for copy in scalars:
        copy.start()

    @pl.loop(1, pieces)
    def _(piece):
        load(0, piece).start()

    @pl.loop(0, pieces)
    def _(piece):
        load(1, piece).start()

    def prepare(side, piece):
        load(side, piece).wait()
        at = block(piece, PIECE)
        full = held[side][at, :].astype(jnp.float32)
        scaled = lax.rsqrt(jnp.sum(full * full, axis=1, keepdims=True) + 1e-06)
        inverse[side][at, :] = scaled
        own[block(piece, PIECE, side * rows), :] = (full * scaled).astype(jnp.bfloat16)

    def send(side, piece):
        to_far(side * pieces + piece).start()
        to_near(side * pieces + piece).start()

    prepare(0, 0)
    pl.semaphore_wait(barrier, 2)
    send(0, 0)
    for side in (0, 1):
        @pl.loop(1 - side, pieces)
        def _(piece):
            prepare(side, piece)
            send(side, piece)

    for copy in scalars:
        copy.wait()
    scale = scale_ref[0, 0]
    bias = bias_ref[0, 0]
    text_factor[...] = scale * text_inv[...]
    image_acc[...] = jnp.zeros_like(image_acc)
    text_acc[...] = jnp.zeros_like(text_acc)
    loss[...] = jnp.zeros_like(loss)

    def products(side, source, step, diagonal=False):
        other = (1 - side) * rows
        here = source[block(step, CHUNK, side * rows), :]
        product = lax.dot_general(
            own[other:other + rows, :], here, (((1,), (1,)), ((), ())), preferred_element_type=jnp.float32
        )
        value = scale * product + bias
        if diagonal:
            row = lax.broadcasted_iota(jnp.int32, value.shape, 0)
            column = lax.broadcasted_iota(jnp.int32, value.shape, 1) + step * CHUNK
            matched = row == column
            value = jnp.where(matched, -value, value)
        small = jnp.exp(-jnp.abs(value))
        slope = jnp.where(value >= 0, 1.0, small) / (1.0 + small)
        if side == 0:
            loss[...] += jnp.maximum(value, 0.0) + jnp.log1p(small)
        if diagonal:
            slope = jnp.where(matched, -slope, slope)
        slope = slope.astype(jnp.bfloat16)
        for start in range(0, width, 384):
            columns = slice(start, min(start + 384, width))
            total[side][:, columns] += jnp.dot(slope, here[:, columns], preferred_element_type=jnp.float32)

    for side in (0, 1):
        @pl.loop(0, rows // CHUNK)
        def _(step):
            products(side, own, step, diagonal=True)

    per = CHUNK // PIECE
    steps = rows // CHUNK

    def arrived(copy, side, step):
        for part in range(per):
            copy(side * pieces + step * per + part).wait_recv()

    def sent(copy, start, stop):
        @pl.loop(start, stop)
        def _(piece):
            copy(piece).wait_send()

    for side in (0, 1):
        @pl.loop(0, steps - side)
        def _(step):
            arrived(to_near, side, step)
            products(side, near, step)
            arrived(to_far, side, step)
            products(side, far, step)

        if side == 0:
            loss_out[...] = jnp.sum(loss[...].T, axis=0) / (3.0 * rows)
            @pl.loop(0, rows // FINISH)
            def _(step):
                at = block(step, FINISH)
                finish(at, image, image_inv, scale * image_inv[at, :], image_acc, image_grad)

    arrived(to_near, 1, steps - 1)
    products(1, near, steps - 1)
    sent(to_far, 0, pieces)
    sent(to_near, 0, 2 * pieces)
    arrived(to_far, 1, steps - 1)
    products(1, far, steps - 1)
    sent(to_far, pieces, 2 * pieces)


def finish(at, emb, inverse, factor, acc, out):
    grad = acc[at, :]
    unit = emb[at, :].astype(jnp.float32) * inverse[at, :]
    along = jnp.sum(unit * grad, axis=1, keepdims=True)
    out[at, :] = ((grad - unit * along) * factor).astype(jnp.bfloat16)


def write(loss, image_grad, text_acc, text, text_inv, text_factor, loss_out, image_out, text_out, text_grad, sem):
    rows = text.shape[0]
    steps = rows // FINISH
    early = [pltpu.make_async_copy(image_grad, image_out, sem.at[steps]), pltpu.make_async_copy(loss, loss_out, sem.at[steps + 1])]
    for copy in early:
        copy.start()
    late = []
    for step in range(steps):
        at = slice(step * FINISH, (step + 1) * FINISH)
        finish(at, text, text_inv, text_factor[at, :], text_acc, text_grad)
        late.append(pltpu.make_async_copy(text_grad.at[at], text_out.at[at], sem.at[step]))
        late[-1].start()
    for copy in early + late:
        copy.wait()


def local(image_emb, text_emb, logit_scale, logit_bias):
    rows, width = image_emb.shape
    n = lax.axis_size("contrast")
    copies = 2 * rows // PIECE
    both = pltpu.VMEM((2 * rows, width), jnp.bfloat16)
    dma = pltpu.SemaphoreType.DMA
    shape = jax.ShapeDtypeStruct
    vmem = pl.BlockSpec(memory_space=pltpu.VMEM)
    hbm = pl.BlockSpec(memory_space=pltpu.HBM)
    handed = pl.pallas_call(
        functools.partial(exchange, n),
        out_shape=(
            shape((rows,), jnp.float32),
            shape((rows, width), jnp.bfloat16),
            shape((rows, width), jnp.float32),
            shape((rows, width), jnp.bfloat16),
            shape((rows, 1), jnp.float32),
            shape((rows, 1), jnp.float32),
        ),
        in_specs=[hbm] * 4,
        out_specs=(vmem,) * 6,
        scratch_shapes=[
            pltpu.VMEM((rows, width), jnp.bfloat16),
            pltpu.VMEM((rows, 1), jnp.float32),
            pltpu.VMEM((rows, width), jnp.float32),
            both,
            both,
            both,
            pltpu.VMEM((rows, CHUNK), jnp.float32),
            pltpu.SMEM((1, 1), jnp.float32),
            pltpu.SMEM((1, 1), jnp.float32),
            dma((2,)),
            dma((copies,)),
            dma((copies,)),
            dma((copies,)),
            dma((copies,)),
            dma((copies,)),
        ],
        compiler_params=pltpu.CompilerParams(
            collective_id=0, has_side_effects=True, vmem_limit_bytes=32 * 2**20
        ),
        cost_estimate=pl.CostEstimate(
            flops=24 * rows * rows * width, bytes_accessed=8 * rows * width, transcendentals=18 * rows * rows
        ),
        name="exchange",
    )(
        logit_scale.reshape(1, 1),
        logit_bias.reshape(1, 1),
        pltpu.with_memory_space_constraint(image_emb, pltpu.HBM),
        pltpu.with_memory_space_constraint(text_emb, pltpu.HBM),
    )
    return pl.pallas_call(
        write,
        out_shape=(
            shape((rows,), jnp.float32),
            shape((rows, width), jnp.bfloat16),
            shape((rows, width), jnp.bfloat16),
        ),
        in_specs=[vmem] * 6,
        out_specs=(hbm,) * 3,
        scratch_shapes=[pltpu.VMEM((rows, width), jnp.bfloat16), dma((rows // FINISH + 2,))],
        compiler_params=pltpu.CompilerParams(vmem_limit_bytes=16 * 2**20),
        cost_estimate=pl.CostEstimate(flops=8 * rows * width, bytes_accessed=12 * rows * width, transcendentals=0),
        name="write",
    )(*handed)


def solution(mesh):
    placed = (P(("dp", "contrast"), None), P(("dp", "contrast"), None), P(), P())
    return jax.shard_map(
        local,
        mesh=mesh,
        in_specs=placed,
        out_specs=(P(("dp", "contrast")), P(("dp", "contrast"), None), P(("dp", "contrast"), None)),
        check_vma=False,
    )
```

```python
import functools

import jax
import jax.numpy as jnp
from jax import lax
from jax.experimental import pallas as pl
from jax.experimental.pallas import tpu as pltpu
from jax.sharding import PartitionSpec as P

MESH = pl.DeviceIdType.MESH
PIECE = 64
CHUNK = 128
FINISH = 64
WRITE = 128


def block(index, size, base=0):
    return pl.ds(pl.multiple_of(base + index * size, size), size)


def exchange(
    n,
    scale_hbm,
    bias_hbm,
    image_hbm,
    text_hbm,
    loss_out,
    image_grad,
    text_grad,
    text,
    text_inv,
    text_acc,
    image,
    image_inv,
    image_acc,
    own,
    far,
    near,
    back,
    loss,
    scale_ref,
    bias_ref,
    scalar_sem,
    load_sem,
    far_send,
    far_recv,
    near_send,
    near_recv,
):
    rows, width = image_hbm.shape
    pieces = rows // PIECE
    me = lax.axis_index("contrast")
    far_id = {"contrast": lax.rem(me + n // 2, n)}
    near_id = {"contrast": me + 1 - 2 * lax.rem(me, 2)}

    barrier = pltpu.get_barrier_semaphore()
    for partner in (far_id, near_id):
        pl.semaphore_signal(barrier, inc=1, device_id=partner, device_id_type=MESH)

    given = (text_hbm, image_hbm)
    held = (text, image)
    inverse = (text_inv, image_inv)
    total = (image_acc, text_acc)

    def load(side, piece):
        at = block(piece, PIECE)
        return pltpu.make_async_copy(given[side].at[at], held[side].at[at], load_sem.at[side * pieces + piece])

    def remote(target, source, at, buffer, to, send_sem, recv_sem, piece):
        return pltpu.make_async_remote_copy(
            src_ref=source.at[at],
            dst_ref=buffer.at[to],
            send_sem=send_sem.at[piece],
            recv_sem=recv_sem.at[piece],
            device_id=target,
            device_id_type=MESH,
        )

    def to_near(piece):
        at = block(piece, PIECE)
        return remote(near_id, own, at, near, at, near_send, near_recv, piece)

    def to_far(piece):
        at = block(piece, PIECE)
        return remote(far_id, own, at, far, at, far_send, far_recv, piece)

    def go_back(piece):
        at = block(piece, PIECE)
        return remote(far_id, back, at, far, block(piece, PIECE, rows), far_send, far_recv, pieces + piece)

    load(0, 0).start()
    scalars = [
        pltpu.make_async_copy(source, target, scalar_sem.at[i])
        for i, (source, target) in enumerate(((scale_hbm, scale_ref), (bias_hbm, bias_ref)))
    ]
    for copy in scalars:
        copy.start()

    @pl.loop(1, pieces)
    def _(piece):
        load(0, piece).start()

    @pl.loop(0, pieces)
    def _(piece):
        load(1, piece).start()

    def prepare(side, piece):
        load(side, piece).wait()
        at = block(piece, PIECE)
        full = held[side][at, :].astype(jnp.float32)
        scaled = lax.rsqrt(jnp.sum(full * full, axis=1, keepdims=True) + 1e-06)
        inverse[side][at, :] = scaled
        own[block(piece, PIECE, side * rows), :] = (full * scaled).astype(jnp.bfloat16)

    prepare(0, 0)
    pl.semaphore_wait(barrier, 2)
    to_far(0).start()
    to_near(0).start()

    @pl.loop(1, pieces)
    def _(piece):
        prepare(0, piece)
        to_far(piece).start()
        to_near(piece).start()

    @pl.loop(0, pieces)
    def _(piece):
        prepare(1, piece)
        to_near(pieces + piece).start()

    for copy in scalars:
        copy.wait()
    scale = scale_ref[0, 0]
    bias = bias_ref[0, 0]
    image_acc[...] = jnp.zeros_like(image_acc)
    text_acc[...] = jnp.zeros_like(text_acc)
    loss[...] = jnp.zeros_like(loss)

    def products(side, source, step, diagonal=False, returned=False):
        other = (1 - side) * rows
        here = source[block(step, CHUNK, side * rows), :]
        product = lax.dot_general(
            own[other:other + rows, :], here, (((1,), (1,)), ((), ())), preferred_element_type=jnp.float32
        )
        value = scale * product + bias
        if diagonal:
            row = lax.broadcasted_iota(jnp.int32, value.shape, 0)
            column = lax.broadcasted_iota(jnp.int32, value.shape, 1) + step * CHUNK
            matched = row == column
            value = jnp.where(matched, -value, value)
        small = jnp.exp(-jnp.abs(value))
        slope = jnp.where(value >= 0, 1.0, small) / (1.0 + small)
        if side == 0:
            loss[...] += jnp.maximum(value, 0.0) + jnp.log1p(small)
        if diagonal:
            slope = jnp.where(matched, -slope, slope)
        slope = slope.astype(jnp.bfloat16)
        for start in range(0, width, 384):
            columns = slice(start, min(start + 384, width))
            total[side][:, columns] += jnp.dot(slope, here[:, columns], preferred_element_type=jnp.float32)
            if returned:
                back[block(step, CHUNK), columns] = lax.dot_general(
                    slope,
                    own[other:other + rows, columns],
                    (((0,), (0,)), ((), ())),
                    preferred_element_type=jnp.float32,
                ).astype(jnp.bfloat16)

    for side in (0, 1):
        @pl.loop(0, rows // CHUNK)
        def _(step):
            products(side, own, step, diagonal=True)

    per = CHUNK // PIECE

    @pl.loop(0, rows // CHUNK)
    def _(step):
        for part in range(per):
            to_far(step * per + part).wait_recv()
        products(0, far, step, returned=True)
        for part in range(per):
            go_back(step * per + part).start()
        for part in range(per):
            to_near(step * per + part).wait_recv()
        products(0, near, step)

    loss_out[...] = jnp.sum(loss[...].T, axis=0) / (3.0 * rows)

    @pl.loop(0, rows // FINISH)
    def _(step):
        at = block(step, FINISH)
        finish(image_acc[at, :], image[at, :], image_inv[at, :], scale, image_grad, at)

    @pl.loop(0, rows // CHUNK)
    def _(step):
        for part in range(per):
            to_near(pieces + step * per + part).wait_recv()
        products(1, near, step)

    @pl.loop(0, pieces)
    def _(piece):
        to_far(piece).wait_send()
        to_near(piece).wait_send()
        to_near(pieces + piece).wait_send()

    @pl.loop(0, pieces)
    def _(piece):
        go_back(piece).wait_recv()
        at = block(piece, PIECE)
        grad = text_acc[at, :] + far[block(piece, PIECE, rows), :].astype(jnp.float32)
        finish(grad, text[at, :], text_inv[at, :], scale, text_grad, at)

    @pl.loop(0, pieces)
    def _(piece):
        go_back(piece).wait_send()


def finish(grad, emb, inverse, scale, out, at):
    unit = emb.astype(jnp.float32) * inverse
    along = jnp.sum(unit * grad, axis=1, keepdims=True)
    out[at, :] = ((grad - unit * along) * (scale * inverse)).astype(jnp.bfloat16)


def write(loss, image_grad, text_grad, loss_out, image_out, text_out, sem):
    rows = image_grad.shape[0]
    copies = [pltpu.make_async_copy(loss, loss_out, sem.at[0])]
    for side, (source, target) in enumerate(((image_grad, image_out), (text_grad, text_out))):
        for step in range(rows // WRITE):
            at = pl.ds(step * WRITE, WRITE)
            copies.append(pltpu.make_async_copy(source.at[at], target.at[at], sem.at[len(copies)]))
    for copy in copies:
        copy.start()
    for copy in copies:
        copy.wait()


def local(image_emb, text_emb, logit_scale, logit_bias):
    rows, width = image_emb.shape
    n = lax.axis_size("contrast")
    copies = 2 * rows // PIECE
    both = pltpu.VMEM((2 * rows, width), jnp.bfloat16)
    dma = pltpu.SemaphoreType.DMA
    shape = jax.ShapeDtypeStruct
    vmem = pl.BlockSpec(memory_space=pltpu.VMEM)
    hbm = pl.BlockSpec(memory_space=pltpu.HBM)
    outs = (shape((rows,), jnp.float32), shape((rows, width), jnp.bfloat16), shape((rows, width), jnp.bfloat16))
    one = pltpu.VMEM((rows, width), jnp.bfloat16)
    wide = pltpu.VMEM((rows, width), jnp.float32)
    column = pltpu.VMEM((rows, 1), jnp.float32)
    handed = pl.pallas_call(
        functools.partial(exchange, n),
        out_shape=outs,
        in_specs=[hbm] * 4,
        out_specs=(vmem,) * 3,
        scratch_shapes=[
            one,
            column,
            wide,
            one,
            column,
            wide,
            both,
            both,
            both,
            one,
            pltpu.VMEM((rows, CHUNK), jnp.float32),
            pltpu.SMEM((1, 1), jnp.float32),
            pltpu.SMEM((1, 1), jnp.float32),
            dma((2,)),
            dma((copies,)),
            dma((copies,)),
            dma((copies,)),
            dma((copies,)),
            dma((copies,)),
        ],
        compiler_params=pltpu.CompilerParams(
            collective_id=0, has_side_effects=True, vmem_limit_bytes=32 * 2**20
        ),
        cost_estimate=pl.CostEstimate(
            flops=22 * rows * rows * width, bytes_accessed=8 * rows * width, transcendentals=15 * rows * rows
        ),
        name="exchange",
    )(
        logit_scale.reshape(1, 1),
        logit_bias.reshape(1, 1),
        pltpu.with_memory_space_constraint(image_emb, pltpu.HBM),
        pltpu.with_memory_space_constraint(text_emb, pltpu.HBM),
    )
    return pl.pallas_call(
        write,
        out_shape=outs,
        in_specs=[vmem] * 3,
        out_specs=(hbm,) * 3,
        scratch_shapes=[dma((2 * rows // WRITE + 1,))],
        compiler_params=pltpu.CompilerParams(vmem_limit_bytes=4 * 2**20),
        cost_estimate=pl.CostEstimate(flops=0, bytes_accessed=8 * rows * width, transcendentals=0),
        name="write",
    )(*handed)


def solution(mesh):
    placed = (P(("dp", "contrast"), None), P(("dp", "contrast"), None), P(), P())
    return jax.shard_map(
        local,
        mesh=mesh,
        in_specs=placed,
        out_specs=(P(("dp", "contrast")), P(("dp", "contrast"), None), P(("dp", "contrast"), None)),
        check_vma=False,
    )
```

```python
import functools

import jax
import jax.numpy as jnp
from jax import lax
from jax.experimental import pallas as pl
from jax.experimental.pallas import tpu as pltpu
from jax.sharding import PartitionSpec as P

MESH = pl.DeviceIdType.MESH
PIECE = 128
TEXT = 128
PREPARE = 64
CHUNK = 128
FINISH = 64
WRITE = 128


def block(index, size, base=0):
    return pl.ds(pl.multiple_of(base + index * size, size), size)


def exchange(
    n,
    scale_hbm,
    bias_hbm,
    image_hbm,
    text_hbm,
    loss_out,
    image_grad,
    text_grad,
    text,
    text_inv,
    text_acc,
    image,
    image_inv,
    image_acc,
    own,
    far,
    near,
    back,
    loss,
    scale_ref,
    bias_ref,
    scalar_sem,
    load_sem,
    far_send,
    far_recv,
    near_send,
    near_recv,
):
    rows, width = image_hbm.shape
    pieces = rows // PIECE
    sends = rows // TEXT
    parts = rows // PREPARE
    me = lax.axis_index("contrast")
    far_id = {"contrast": lax.rem(me + n // 2, n)}
    near_id = {"contrast": me + 1 - 2 * lax.rem(me, 2)}

    barrier = pltpu.get_barrier_semaphore()
    for partner in (far_id, near_id):
        pl.semaphore_signal(barrier, inc=1, device_id=partner, device_id_type=MESH)

    given = (text_hbm, image_hbm)
    held = (text, image)
    inverse = (text_inv, image_inv)
    total = (image_acc, text_acc)

    def remote(target, source, at, buffer, to, send_sem, recv_sem, piece):
        return pltpu.make_async_remote_copy(
            src_ref=source.at[at],
            dst_ref=buffer.at[to],
            send_sem=send_sem.at[piece],
            recv_sem=recv_sem.at[piece],
            device_id=target,
            device_id_type=MESH,
        )

    def to_near(piece):
        at = block(piece, TEXT)
        return remote(near_id, own, at, near, at, near_send, near_recv, piece)

    def to_far(piece):
        at = block(piece, TEXT)
        return remote(far_id, text_hbm, at, far, at, far_send, far_recv, piece)

    def go_back(piece):
        at = block(piece, PIECE)
        return remote(far_id, back, at, far, block(piece, PIECE, rows), far_send, far_recv, sends + piece)

    def load(side, piece):
        at = block(piece, PREPARE)
        return pltpu.make_async_copy(given[side].at[at], held[side].at[at], load_sem.at[side * parts + piece])

    for side in (0, 1):
        @pl.loop(0, parts)
        def _(piece):
            load(side, piece).start()

    scalars = [
        pltpu.make_async_copy(source, target, scalar_sem.at[i])
        for i, (source, target) in enumerate(((scale_hbm, scale_ref), (bias_hbm, bias_ref)))
    ]
    for copy in scalars:
        copy.start()

    pl.semaphore_wait(barrier, 2)

    @pl.loop(0, sends)
    def _(piece):
        to_far(piece).start()

    def prepare(side, piece):
        load(side, piece).wait()
        at = block(piece, PREPARE)
        unit, scaled = normalize(held[side][at, :])
        inverse[side][at, :] = scaled
        own[block(piece, PREPARE, side * rows), :] = unit

    per_send = TEXT // PREPARE

    @pl.loop(0, sends)
    def _(piece):
        @pl.loop(0, per_send)
        def _(part):
            prepare(0, piece * per_send + part)

        to_near(piece).start()

    @pl.loop(0, sends)
    def _(piece):
        @pl.loop(0, per_send)
        def _(part):
            prepare(1, piece * per_send + part)

        to_near(sends + piece).start()

    for copy in scalars:
        copy.wait()
    scale = scale_ref[0, 0]
    bias = bias_ref[0, 0]
    image_acc[...] = jnp.zeros_like(image_acc)
    text_acc[...] = jnp.zeros_like(text_acc)
    loss[...] = jnp.zeros_like(loss)

    def products(side, source, step, diagonal=False, returned=False):
        other = (1 - side) * rows
        here = source[block(step, CHUNK, side * rows), :]
        if returned:
            here, _ = normalize(here)
        product = lax.dot_general(
            own[other:other + rows, :], here, (((1,), (1,)), ((), ())), preferred_element_type=jnp.float32
        )
        value = scale * product + bias
        if diagonal:
            row = lax.broadcasted_iota(jnp.int32, value.shape, 0)
            column = lax.broadcasted_iota(jnp.int32, value.shape, 1) + step * CHUNK
            matched = row == column
            value = jnp.where(matched, -value, value)
        small = jnp.exp(-jnp.abs(value))
        slope = jnp.where(value >= 0, 1.0, small) / (1.0 + small)
        if side == 0:
            loss[...] += jnp.maximum(value, 0.0) + jnp.log1p(small)
        if diagonal:
            slope = jnp.where(matched, -slope, slope)
        slope = slope.astype(jnp.bfloat16)
        for start in range(0, width, 384):
            columns = slice(start, min(start + 384, width))
            total[side][:, columns] += jnp.dot(slope, here[:, columns], preferred_element_type=jnp.float32)
            if returned:
                back[block(step, CHUNK), columns] = lax.dot_general(
                    slope,
                    own[other:other + rows, columns],
                    (((0,), (0,)), ((), ())),
                    preferred_element_type=jnp.float32,
                ).astype(jnp.bfloat16)

    for side in (0, 1):
        @pl.loop(0, rows // CHUNK)
        def _(step):
            products(side, own, step, diagonal=True)

    per = CHUNK // PIECE
    steps = TEXT // CHUNK

    @pl.loop(0, sends)
    def _(piece):
        to_far(piece).wait_recv()

        @pl.loop(piece * steps, (piece + 1) * steps)
        def _(step):
            products(0, far, step, returned=True)
            for part in range(per):
                go_back(step * per + part).start()

        to_near(piece).wait_recv()

        @pl.loop(piece * steps, (piece + 1) * steps)
        def _(step):
            products(0, near, step)

    loss_out[...] = jnp.sum(loss[...].T, axis=0) / (3.0 * rows)

    @pl.loop(0, rows // FINISH)
    def _(step):
        at = block(step, FINISH)
        finish(image_acc[at, :], image[at, :], image_inv[at, :], scale, image_grad, at)

    @pl.loop(0, sends)
    def _(piece):
        to_near(sends + piece).wait_recv()

        @pl.loop(piece * steps, (piece + 1) * steps)
        def _(step):
            products(1, near, step)

    @pl.loop(0, sends)
    def _(piece):
        to_far(piece).wait_send()
        to_near(piece).wait_send()
        to_near(sends + piece).wait_send()

    @pl.loop(0, pieces)
    def _(piece):
        go_back(piece).wait_recv()
        at = block(piece, PIECE)
        grad = text_acc[at, :] + far[block(piece, PIECE, rows), :].astype(jnp.float32)
        finish(grad, text[at, :], text_inv[at, :], scale, text_grad, at)

    @pl.loop(0, pieces)
    def _(piece):
        go_back(piece).wait_send()


def normalize(emb):
    full = emb.astype(jnp.float32)
    scaled = lax.rsqrt(jnp.sum(full * full, axis=1, keepdims=True) + 1e-06)
    return (full * scaled).astype(jnp.bfloat16), scaled


def finish(grad, emb, inverse, scale, out, at):
    unit = emb.astype(jnp.float32) * inverse
    along = jnp.sum(unit * grad, axis=1, keepdims=True)
    out[at, :] = ((grad - unit * along) * (scale * inverse)).astype(jnp.bfloat16)


def write(loss, image_grad, text_grad, loss_out, image_out, text_out, sem):
    rows = image_grad.shape[0]
    copies = [pltpu.make_async_copy(loss, loss_out, sem.at[0])]
    for side, (source, target) in enumerate(((image_grad, image_out), (text_grad, text_out))):
        for step in range(rows // WRITE):
            at = pl.ds(step * WRITE, WRITE)
            copies.append(pltpu.make_async_copy(source.at[at], target.at[at], sem.at[len(copies)]))
    for copy in copies:
        copy.start()
    for copy in copies:
        copy.wait()


def local(image_emb, text_emb, logit_scale, logit_bias):
    rows, width = image_emb.shape
    n = lax.axis_size("contrast")
    sends = rows // TEXT
    copies = sends + rows // PIECE
    both = pltpu.VMEM((2 * rows, width), jnp.bfloat16)
    dma = pltpu.SemaphoreType.DMA
    shape = jax.ShapeDtypeStruct
    vmem = pl.BlockSpec(memory_space=pltpu.VMEM)
    hbm = pl.BlockSpec(memory_space=pltpu.HBM)
    outs = (shape((rows,), jnp.float32), shape((rows, width), jnp.bfloat16), shape((rows, width), jnp.bfloat16))
    one = pltpu.VMEM((rows, width), jnp.bfloat16)
    wide = pltpu.VMEM((rows, width), jnp.float32)
    column = pltpu.VMEM((rows, 1), jnp.float32)
    handed = pl.pallas_call(
        functools.partial(exchange, n),
        out_shape=outs,
        in_specs=[hbm] * 4,
        out_specs=(vmem,) * 3,
        scratch_shapes=[
            one,
            column,
            wide,
            one,
            column,
            wide,
            both,
            both,
            both,
            one,
            pltpu.VMEM((rows, CHUNK), jnp.float32),
            pltpu.SMEM((1, 1), jnp.float32),
            pltpu.SMEM((1, 1), jnp.float32),
            dma((2,)),
            dma((2 * rows // PREPARE,)),
            dma((copies,)),
            dma((copies,)),
            dma((2 * sends,)),
            dma((2 * sends,)),
        ],
        compiler_params=pltpu.CompilerParams(
            collective_id=0, has_side_effects=True, vmem_limit_bytes=32 * 2**20
        ),
        cost_estimate=pl.CostEstimate(
            flops=22 * rows * rows * width, bytes_accessed=8 * rows * width, transcendentals=15 * rows * rows
        ),
        name="exchange",
    )(
        logit_scale.reshape(1, 1),
        logit_bias.reshape(1, 1),
        pltpu.with_memory_space_constraint(image_emb, pltpu.HBM),
        pltpu.with_memory_space_constraint(text_emb, pltpu.HBM),
    )
    return pl.pallas_call(
        write,
        out_shape=outs,
        in_specs=[vmem] * 3,
        out_specs=(hbm,) * 3,
        scratch_shapes=[dma((2 * rows // WRITE + 1,))],
        compiler_params=pltpu.CompilerParams(vmem_limit_bytes=4 * 2**20),
        cost_estimate=pl.CostEstimate(flops=0, bytes_accessed=8 * rows * width, transcendentals=0),
        name="write",
    )(*handed)


def solution(mesh):
    placed = (P(("dp", "contrast"), None), P(("dp", "contrast"), None), P(), P())
    return jax.shard_map(
        local,
        mesh=mesh,
        in_specs=placed,
        out_specs=(P(("dp", "contrast")), P(("dp", "contrast"), None), P(("dp", "contrast"), None)),
        check_vma=False,
    )
```

```python
import functools

import jax
import jax.numpy as jnp
from jax import lax
from jax.experimental import pallas as pl
from jax.experimental.pallas import tpu as pltpu
from jax.sharding import PartitionSpec as P

MESH = pl.DeviceIdType.MESH
PIECE = 128
TEXT = 128
PREPARE = 64
CHUNK = 128
FINISH = 64
WRITE = 256


def block(index, size, base=0):
    return pl.ds(pl.multiple_of(base + index * size, size), size)


def exchange(
    n,
    scale_hbm,
    bias_hbm,
    image_hbm,
    text_hbm,
    loss_out,
    image_grad,
    text_grad,
    text,
    text_inv,
    text_acc,
    image,
    image_inv,
    image_acc,
    own,
    far,
    near,
    back,
    loss,
    scale_ref,
    bias_ref,
    scalar_sem,
    load_sem,
    far_send,
    far_recv,
    near_send,
    near_recv,
):
    rows, width = image_hbm.shape
    pieces = rows // PIECE
    sends = rows // TEXT
    parts = rows // PREPARE
    me = lax.axis_index("contrast")
    far_id = {"contrast": lax.rem(me + n // 2, n)}
    near_id = {"contrast": me + 1 - 2 * lax.rem(me, 2)}

    barrier = pltpu.get_barrier_semaphore()
    for partner in (far_id, near_id):
        pl.semaphore_signal(barrier, inc=1, device_id=partner, device_id_type=MESH)

    given = (text_hbm, image_hbm)
    held = (text, image)
    inverse = (text_inv, image_inv)
    total = (image_acc, text_acc)

    def remote(target, source, at, buffer, to, send_sem, recv_sem, piece):
        return pltpu.make_async_remote_copy(
            src_ref=source.at[at],
            dst_ref=buffer.at[to],
            send_sem=send_sem.at[piece],
            recv_sem=recv_sem.at[piece],
            device_id=target,
            device_id_type=MESH,
        )

    def to_near(piece):
        at = block(piece, TEXT)
        return remote(near_id, own, at, near, at, near_send, near_recv, piece)

    def to_far(piece):
        at = block(piece, TEXT)
        return remote(far_id, text_hbm, at, far, at, far_send, far_recv, piece)

    def go_back(piece):
        at = block(piece, PIECE)
        return remote(far_id, back, at, far, block(piece, PIECE, rows), far_send, far_recv, sends + piece)

    pl.semaphore_wait(barrier, 2)

    @pl.loop(0, sends)
    def _(piece):
        to_far(piece).start()

    def load(side, piece):
        at = block(piece, PREPARE)
        return pltpu.make_async_copy(given[side].at[at], held[side].at[at], load_sem.at[side * parts + piece])

    for side in (0, 1):
        @pl.loop(0, parts)
        def _(piece):
            load(side, piece).start()

    scalars = [
        pltpu.make_async_copy(source, target, scalar_sem.at[i])
        for i, (source, target) in enumerate(((scale_hbm, scale_ref), (bias_hbm, bias_ref)))
    ]
    for copy in scalars:
        copy.start()

    def prepare(side, piece):
        load(side, piece).wait()
        at = block(piece, PREPARE)
        unit, scaled = normalize(held[side][at, :])
        inverse[side][at, :] = scaled
        own[block(piece, PREPARE, side * rows), :] = unit

    per_send = TEXT // PREPARE

    @pl.loop(0, sends)
    def _(piece):
        @pl.loop(0, per_send)
        def _(part):
            prepare(0, piece * per_send + part)

        to_near(piece).start()

    @pl.loop(0, sends)
    def _(piece):
        @pl.loop(0, per_send)
        def _(part):
            prepare(1, piece * per_send + part)

        to_near(sends + piece).start()

    for copy in scalars:
        copy.wait()
    scale = scale_ref[0, 0]
    bias = bias_ref[0, 0]
    image_acc[...] = jnp.zeros_like(image_acc)
    text_acc[...] = jnp.zeros_like(text_acc)
    loss[...] = jnp.zeros_like(loss)

    def products(side, source, step, diagonal=False, returned=False):
        other = (1 - side) * rows
        here = source[block(step, CHUNK, side * rows), :]
        if returned:
            here, _ = normalize(here)
        product = lax.dot_general(
            own[other:other + rows, :], here, (((1,), (1,)), ((), ())), preferred_element_type=jnp.float32
        )
        value = scale * product + bias
        if diagonal:
            row = lax.broadcasted_iota(jnp.int32, value.shape, 0)
            column = lax.broadcasted_iota(jnp.int32, value.shape, 1) + step * CHUNK
            matched = row == column
            value = jnp.where(matched, -value, value)
        small = jnp.exp(-jnp.abs(value))
        slope = jnp.where(value >= 0, 1.0, small) / (1.0 + small)
        if side == 0:
            loss[...] += jnp.maximum(value, 0.0) + jnp.log1p(small)
        if diagonal:
            slope = jnp.where(matched, -slope, slope)
        slope = slope.astype(jnp.bfloat16)
        for start in range(0, width, 384):
            columns = slice(start, min(start + 384, width))
            total[side][:, columns] += jnp.dot(slope, here[:, columns], preferred_element_type=jnp.float32)
            if returned:
                back[block(step, CHUNK), columns] = lax.dot_general(
                    slope,
                    own[other:other + rows, columns],
                    (((0,), (0,)), ((), ())),
                    preferred_element_type=jnp.float32,
                ).astype(jnp.bfloat16)

    for side in (0, 1):
        @pl.loop(0, rows // CHUNK)
        def _(step):
            products(side, own, step, diagonal=True)

    per = CHUNK // PIECE
    steps = TEXT // CHUNK

    @pl.loop(0, sends)
    def _(piece):
        to_far(piece).wait_recv()

        @pl.loop(piece * steps, (piece + 1) * steps)
        def _(step):
            products(0, far, step, returned=True)
            for part in range(per):
                go_back(step * per + part).start()

        to_near(piece).wait_recv()

        @pl.loop(piece * steps, (piece + 1) * steps)
        def _(step):
            products(0, near, step)

    loss_out[...] = jnp.sum(loss[...].T, axis=0) / (3.0 * rows)

    @pl.loop(0, rows // FINISH)
    def _(step):
        at = block(step, FINISH)
        finish(image_acc[at, :], image[at, :], image_inv[at, :], scale, image_grad, at)

    @pl.loop(0, sends)
    def _(piece):
        to_near(sends + piece).wait_recv()

        @pl.loop(piece * steps, (piece + 1) * steps)
        def _(step):
            products(1, near, step)

    @pl.loop(0, sends)
    def _(piece):
        to_far(piece).wait_send()
        to_near(piece).wait_send()
        to_near(sends + piece).wait_send()

    @pl.loop(0, pieces)
    def _(piece):
        go_back(piece).wait_recv()
        at = block(piece, PIECE)
        grad = text_acc[at, :] + far[block(piece, PIECE, rows), :].astype(jnp.float32)
        finish(grad, text[at, :], text_inv[at, :], scale, text_grad, at)

    @pl.loop(0, pieces)
    def _(piece):
        go_back(piece).wait_send()


def normalize(emb):
    full = emb.astype(jnp.float32)
    scaled = lax.rsqrt(jnp.sum(full * full, axis=1, keepdims=True) + 1e-06)
    return (full * scaled).astype(jnp.bfloat16), scaled


def finish(grad, emb, inverse, scale, out, at):
    unit = emb.astype(jnp.float32) * inverse
    along = jnp.sum(unit * grad, axis=1, keepdims=True)
    out[at, :] = ((grad - unit * along) * (scale * inverse)).astype(jnp.bfloat16)


def write(loss, image_grad, text_grad, loss_out, image_out, text_out, sem):
    rows = image_grad.shape[0]
    copies = [pltpu.make_async_copy(loss, loss_out, sem.at[0])]
    for side, (source, target) in enumerate(((image_grad, image_out), (text_grad, text_out))):
        for step in range(rows // WRITE):
            at = pl.ds(step * WRITE, WRITE)
            copies.append(pltpu.make_async_copy(source.at[at], target.at[at], sem.at[len(copies)]))
    for copy in copies:
        copy.start()
    for copy in copies:
        copy.wait()


def local(image_emb, text_emb, logit_scale, logit_bias):
    rows, width = image_emb.shape
    n = lax.axis_size("contrast")
    sends = rows // TEXT
    copies = sends + rows // PIECE
    both = pltpu.VMEM((2 * rows, width), jnp.bfloat16)
    dma = pltpu.SemaphoreType.DMA
    shape = jax.ShapeDtypeStruct
    vmem = pl.BlockSpec(memory_space=pltpu.VMEM)
    hbm = pl.BlockSpec(memory_space=pltpu.HBM)
    outs = (shape((rows,), jnp.float32), shape((rows, width), jnp.bfloat16), shape((rows, width), jnp.bfloat16))
    one = pltpu.VMEM((rows, width), jnp.bfloat16)
    wide = pltpu.VMEM((rows, width), jnp.float32)
    column = pltpu.VMEM((rows, 1), jnp.float32)
    handed = pl.pallas_call(
        functools.partial(exchange, n),
        out_shape=outs,
        in_specs=[hbm] * 4,
        out_specs=(vmem,) * 3,
        scratch_shapes=[
            one,
            column,
            wide,
            one,
            column,
            wide,
            both,
            both,
            both,
            one,
            pltpu.VMEM((rows, CHUNK), jnp.float32),
            pltpu.SMEM((1, 1), jnp.float32),
            pltpu.SMEM((1, 1), jnp.float32),
            dma((2,)),
            dma((2 * rows // PREPARE,)),
            dma((copies,)),
            dma((copies,)),
            dma((2 * sends,)),
            dma((2 * sends,)),
        ],
        compiler_params=pltpu.CompilerParams(
            collective_id=0, has_side_effects=True, vmem_limit_bytes=32 * 2**20
        ),
        cost_estimate=pl.CostEstimate(
            flops=22 * rows * rows * width, bytes_accessed=8 * rows * width, transcendentals=15 * rows * rows
        ),
        name="exchange",
    )(
        logit_scale.reshape(1, 1),
        logit_bias.reshape(1, 1),
        pltpu.with_memory_space_constraint(image_emb, pltpu.HBM),
        pltpu.with_memory_space_constraint(text_emb, pltpu.HBM),
    )
    return pl.pallas_call(
        write,
        out_shape=outs,
        in_specs=[vmem] * 3,
        out_specs=(hbm,) * 3,
        scratch_shapes=[dma((2 * rows // WRITE + 1,))],
        compiler_params=pltpu.CompilerParams(vmem_limit_bytes=4 * 2**20),
        cost_estimate=pl.CostEstimate(flops=0, bytes_accessed=8 * rows * width, transcendentals=0),
        name="write",
    )(*handed)


def solution(mesh):
    placed = (P(("dp", "contrast"), None), P(("dp", "contrast"), None), P(), P())
    return jax.shard_map(
        local,
        mesh=mesh,
        in_specs=placed,
        out_specs=(P(("dp", "contrast")), P(("dp", "contrast"), None), P(("dp", "contrast"), None)),
        check_vma=False,
    )
```

```python
import functools

import jax
import jax.numpy as jnp
from jax import lax
from jax.experimental import pallas as pl
from jax.experimental.pallas import tpu as pltpu
from jax.sharding import PartitionSpec as P

MESH = pl.DeviceIdType.MESH
PIECE = 128
TEXT = 256
PREPARE = 64
CHUNK = 128
FINISH = 64
WRITE = 512


def block(index, size, base=0):
    return pl.ds(pl.multiple_of(base + index * size, size), size)


def exchange(
    n,
    scale_hbm,
    bias_hbm,
    image_hbm,
    text_hbm,
    loss_out,
    image_grad,
    text_grad,
    text,
    text_inv,
    text_acc,
    image,
    image_inv,
    image_acc,
    own,
    far,
    near,
    back,
    loss,
    scale_ref,
    bias_ref,
    scalar_sem,
    load_sem,
    far_send,
    far_recv,
    near_send,
    near_recv,
):
    rows, width = image_hbm.shape
    pieces = rows // PIECE
    sends = rows // TEXT
    parts = rows // PREPARE
    me = lax.axis_index("contrast")
    far_id = {"contrast": lax.rem(me + n // 2, n)}
    near_id = {"contrast": me + 1 - 2 * lax.rem(me, 2)}

    barrier = pltpu.get_barrier_semaphore()
    for partner in (far_id, near_id):
        pl.semaphore_signal(barrier, inc=1, device_id=partner, device_id_type=MESH)

    given = (text_hbm, image_hbm)
    held = (text, image)
    inverse = (text_inv, image_inv)
    total = (image_acc, text_acc)

    def remote(target, source, at, buffer, to, send_sem, recv_sem, piece):
        return pltpu.make_async_remote_copy(
            src_ref=source.at[at],
            dst_ref=buffer.at[to],
            send_sem=send_sem.at[piece],
            recv_sem=recv_sem.at[piece],
            device_id=target,
            device_id_type=MESH,
        )

    def to_near(piece):
        at = block(piece, TEXT)
        return remote(near_id, own, at, near, at, near_send, near_recv, piece)

    def to_far(piece):
        at = block(piece, TEXT)
        return remote(far_id, text_hbm, at, far, at, far_send, far_recv, piece)

    def go_back(piece):
        at = block(piece, PIECE)
        return remote(far_id, back, at, far, block(piece, PIECE, rows), far_send, far_recv, sends + piece)

    def load(side, piece):
        at = block(piece, PREPARE)
        return pltpu.make_async_copy(given[side].at[at], held[side].at[at], load_sem.at[side * parts + piece])

    for side in (0, 1):
        @pl.loop(0, parts)
        def _(piece):
            load(side, piece).start()

    scalars = [
        pltpu.make_async_copy(source, target, scalar_sem.at[i])
        for i, (source, target) in enumerate(((scale_hbm, scale_ref), (bias_hbm, bias_ref)))
    ]
    for copy in scalars:
        copy.start()

    pl.semaphore_wait(barrier, 2)

    @pl.loop(0, sends)
    def _(piece):
        to_far(piece).start()

    def prepare(side, piece):
        load(side, piece).wait()
        at = block(piece, PREPARE)
        unit, scaled = normalize(held[side][at, :])
        inverse[side][at, :] = scaled
        own[block(piece, PREPARE, side * rows), :] = unit

    per_send = TEXT // PREPARE

    @pl.loop(0, sends)
    def _(piece):
        @pl.loop(0, per_send)
        def _(part):
            prepare(0, piece * per_send + part)

        to_near(piece).start()

    @pl.loop(0, sends)
    def _(piece):
        @pl.loop(0, per_send)
        def _(part):
            prepare(1, piece * per_send + part)

        to_near(sends + piece).start()

    for copy in scalars:
        copy.wait()
    scale = scale_ref[0, 0]
    bias = bias_ref[0, 0]
    image_acc[...] = jnp.zeros_like(image_acc)
    text_acc[...] = jnp.zeros_like(text_acc)
    loss[...] = jnp.zeros_like(loss)

    def products(side, source, step, diagonal=False, returned=False):
        other = (1 - side) * rows
        here = source[block(step, CHUNK, side * rows), :]
        if returned:
            here, _ = normalize(here)
        product = lax.dot_general(
            own[other:other + rows, :], here, (((1,), (1,)), ((), ())), preferred_element_type=jnp.float32
        )
        value = scale * product + bias
        if diagonal:
            row = lax.broadcasted_iota(jnp.int32, value.shape, 0)
            column = lax.broadcasted_iota(jnp.int32, value.shape, 1) + step * CHUNK
            matched = row == column
            value = jnp.where(matched, -value, value)
        small = jnp.exp(-jnp.abs(value))
        slope = jnp.where(value >= 0, 1.0, small) / (1.0 + small)
        if side == 0:
            loss[...] += jnp.maximum(value, 0.0) + jnp.log1p(small)
        if diagonal:
            slope = jnp.where(matched, -slope, slope)
        slope = slope.astype(jnp.bfloat16)
        for start in range(0, width, 384):
            columns = slice(start, min(start + 384, width))
            total[side][:, columns] += jnp.dot(slope, here[:, columns], preferred_element_type=jnp.float32)
            if returned:
                back[block(step, CHUNK), columns] = lax.dot_general(
                    slope,
                    own[other:other + rows, columns],
                    (((0,), (0,)), ((), ())),
                    preferred_element_type=jnp.float32,
                ).astype(jnp.bfloat16)

    for side in (0, 1):
        @pl.loop(0, rows // CHUNK)
        def _(step):
            products(side, own, step, diagonal=True)

    per = CHUNK // PIECE
    steps = TEXT // CHUNK

    @pl.loop(0, sends)
    def _(piece):
        to_far(piece).wait_recv()

        @pl.loop(piece * steps, (piece + 1) * steps)
        def _(step):
            products(0, far, step, returned=True)
            for part in range(per):
                go_back(step * per + part).start()

        to_near(piece).wait_recv()

        @pl.loop(piece * steps, (piece + 1) * steps)
        def _(step):
            products(0, near, step)

    loss_out[...] = jnp.sum(loss[...].T, axis=0) / (3.0 * rows)

    @pl.loop(0, rows // FINISH)
    def _(step):
        at = block(step, FINISH)
        finish(image_acc[at, :], image[at, :], image_inv[at, :], scale, image_grad, at)

    @pl.loop(0, sends)
    def _(piece):
        to_near(sends + piece).wait_recv()

        @pl.loop(piece * steps, (piece + 1) * steps)
        def _(step):
            products(1, near, step)

    @pl.loop(0, sends)
    def _(piece):
        to_far(piece).wait_send()
        to_near(piece).wait_send()
        to_near(sends + piece).wait_send()

    @pl.loop(0, pieces)
    def _(piece):
        go_back(piece).wait_recv()
        at = block(piece, PIECE)
        grad = text_acc[at, :] + far[block(piece, PIECE, rows), :].astype(jnp.float32)
        finish(grad, text[at, :], text_inv[at, :], scale, text_grad, at)

    @pl.loop(0, pieces)
    def _(piece):
        go_back(piece).wait_send()


def normalize(emb):
    full = emb.astype(jnp.float32)
    scaled = lax.rsqrt(jnp.sum(full * full, axis=1, keepdims=True) + 1e-06)
    return (full * scaled).astype(jnp.bfloat16), scaled


def finish(grad, emb, inverse, scale, out, at):
    unit = emb.astype(jnp.float32) * inverse
    along = jnp.sum(unit * grad, axis=1, keepdims=True)
    out[at, :] = ((grad - unit * along) * (scale * inverse)).astype(jnp.bfloat16)


def write(loss, image_grad, text_grad, loss_out, image_out, text_out, sem):
    rows = image_grad.shape[0]
    copies = [pltpu.make_async_copy(loss, loss_out, sem.at[0])]
    for side, (source, target) in enumerate(((image_grad, image_out), (text_grad, text_out))):
        for step in range(rows // WRITE):
            at = pl.ds(step * WRITE, WRITE)
            copies.append(pltpu.make_async_copy(source.at[at], target.at[at], sem.at[len(copies)]))
    for copy in copies:
        copy.start()
    for copy in copies:
        copy.wait()


def local(image_emb, text_emb, logit_scale, logit_bias):
    rows, width = image_emb.shape
    n = lax.axis_size("contrast")
    sends = rows // TEXT
    copies = sends + rows // PIECE
    both = pltpu.VMEM((2 * rows, width), jnp.bfloat16)
    dma = pltpu.SemaphoreType.DMA
    shape = jax.ShapeDtypeStruct
    vmem = pl.BlockSpec(memory_space=pltpu.VMEM)
    hbm = pl.BlockSpec(memory_space=pltpu.HBM)
    outs = (shape((rows,), jnp.float32), shape((rows, width), jnp.bfloat16), shape((rows, width), jnp.bfloat16))
    one = pltpu.VMEM((rows, width), jnp.bfloat16)
    wide = pltpu.VMEM((rows, width), jnp.float32)
    column = pltpu.VMEM((rows, 1), jnp.float32)
    handed = pl.pallas_call(
        functools.partial(exchange, n),
        out_shape=outs,
        in_specs=[hbm] * 4,
        out_specs=(vmem,) * 3,
        scratch_shapes=[
            one,
            column,
            wide,
            one,
            column,
            wide,
            both,
            both,
            both,
            one,
            pltpu.VMEM((rows, CHUNK), jnp.float32),
            pltpu.SMEM((1, 1), jnp.float32),
            pltpu.SMEM((1, 1), jnp.float32),
            dma((2,)),
            dma((2 * rows // PREPARE,)),
            dma((copies,)),
            dma((copies,)),
            dma((2 * sends,)),
            dma((2 * sends,)),
        ],
        compiler_params=pltpu.CompilerParams(
            collective_id=0, has_side_effects=True, vmem_limit_bytes=32 * 2**20
        ),
        cost_estimate=pl.CostEstimate(
            flops=22 * rows * rows * width, bytes_accessed=8 * rows * width, transcendentals=15 * rows * rows
        ),
        name="exchange",
    )(
        logit_scale.reshape(1, 1),
        logit_bias.reshape(1, 1),
        pltpu.with_memory_space_constraint(image_emb, pltpu.HBM),
        pltpu.with_memory_space_constraint(text_emb, pltpu.HBM),
    )
    return pl.pallas_call(
        write,
        out_shape=outs,
        in_specs=[vmem] * 3,
        out_specs=(hbm,) * 3,
        scratch_shapes=[dma((2 * rows // WRITE + 1,))],
        compiler_params=pltpu.CompilerParams(vmem_limit_bytes=4 * 2**20),
        cost_estimate=pl.CostEstimate(flops=0, bytes_accessed=8 * rows * width, transcendentals=0),
        name="write",
    )(*handed)


def solution(mesh):
    placed = (P(("dp", "contrast"), None), P(("dp", "contrast"), None), P(), P())
    return jax.shard_map(
        local,
        mesh=mesh,
        in_specs=placed,
        out_specs=(P(("dp", "contrast")), P(("dp", "contrast"), None), P(("dp", "contrast"), None)),
        check_vma=False,
    )
```

```python
import functools

import jax
import jax.numpy as jnp
from jax import lax
from jax.experimental import pallas as pl
from jax.experimental.pallas import tpu as pltpu
from jax.sharding import PartitionSpec as P

MESH = pl.DeviceIdType.MESH
PIECE = 128
TEXT = 128
PREPARE = 64
CHUNK = 128
FINISH = 64
WRITE = 128


def block(index, size, base=0):
    return pl.ds(pl.multiple_of(base + index * size, size), size)


def exchange(
    n,
    scale_hbm,
    bias_hbm,
    image_hbm,
    text_hbm,
    loss_out,
    image_grad,
    text_grad,
    text,
    text_inv,
    text_acc,
    image,
    image_inv,
    image_acc,
    own,
    far,
    near,
    back,
    loss,
    scale_ref,
    bias_ref,
    scalar_sem,
    load_sem,
    far_send,
    far_recv,
    near_send,
    near_recv,
):
    rows, width = image_hbm.shape
    pieces = rows // PIECE
    sends = rows // TEXT
    parts = rows // PREPARE
    me = lax.axis_index("contrast")
    far_id = {"contrast": lax.rem(me + n // 2, n)}
    near_id = {"contrast": me + 1 - 2 * lax.rem(me, 2)}

    barrier = pltpu.get_barrier_semaphore()
    for partner in (far_id, near_id):
        pl.semaphore_signal(barrier, inc=1, device_id=partner, device_id_type=MESH)

    given = (text_hbm, image_hbm)
    held = (text, image)
    inverse = (text_inv, image_inv)
    total = (image_acc, text_acc)

    def remote(target, source, at, buffer, to, send_sem, recv_sem, piece):
        return pltpu.make_async_remote_copy(
            src_ref=source.at[at],
            dst_ref=buffer.at[to],
            send_sem=send_sem.at[piece],
            recv_sem=recv_sem.at[piece],
            device_id=target,
            device_id_type=MESH,
        )

    def to_near(piece):
        at = block(piece, TEXT)
        return remote(near_id, own, at, near, at, near_send, near_recv, piece)

    def to_far(piece):
        at = block(piece, TEXT)
        return remote(far_id, text_hbm, at, far, at, far_send, far_recv, piece)

    def go_back(piece):
        at = block(piece, PIECE)
        return remote(far_id, back, at, far, block(piece, PIECE, rows), far_send, far_recv, sends + piece)

    def load(side, piece):
        at = block(piece, PREPARE)
        return pltpu.make_async_copy(given[side].at[at], held[side].at[at], load_sem.at[side * parts + piece])

    for side in (0, 1):
        @pl.loop(0, parts)
        def _(piece):
            load(side, piece).start()

    scalars = [
        pltpu.make_async_copy(source, target, scalar_sem.at[i])
        for i, (source, target) in enumerate(((scale_hbm, scale_ref), (bias_hbm, bias_ref)))
    ]
    for copy in scalars:
        copy.start()

    pl.semaphore_wait(barrier, 2)

    @pl.loop(0, sends)
    def _(piece):
        to_far(piece).start()

    def prepare(side, piece):
        load(side, piece).wait()
        at = block(piece, PREPARE)
        unit, scaled = normalize(held[side][at, :])
        inverse[side][at, :] = scaled
        own[block(piece, PREPARE, side * rows), :] = unit

    per_send = TEXT // PREPARE

    @pl.loop(0, sends)
    def _(piece):
        @pl.loop(0, per_send)
        def _(part):
            prepare(0, piece * per_send + part)

        to_near(piece).start()

    @pl.loop(0, sends)
    def _(piece):
        @pl.loop(0, per_send)
        def _(part):
            prepare(1, piece * per_send + part)

        to_near(sends + piece).start()

    for copy in scalars:
        copy.wait()
    scale = scale_ref[0, 0]
    bias = bias_ref[0, 0]
    image_acc[...] = jnp.zeros_like(image_acc)
    text_acc[...] = jnp.zeros_like(text_acc)
    loss[...] = jnp.zeros_like(loss)

    def products(side, source, step, diagonal=False, returned=False):
        other = (1 - side) * rows
        here = source[block(step, CHUNK, side * rows), :]
        if returned:
            here, _ = normalize(here)
        product = lax.dot_general(
            own[other:other + rows, :], here, (((1,), (1,)), ((), ())), preferred_element_type=jnp.float32
        )
        value = scale * product + bias
        if diagonal:
            row = lax.broadcasted_iota(jnp.int32, value.shape, 0)
            column = lax.broadcasted_iota(jnp.int32, value.shape, 1) + step * CHUNK
            matched = row == column
            value = jnp.where(matched, -value, value)
        small = jnp.exp(-jnp.abs(value))
        slope = jnp.where(value >= 0, 1.0, small) / (1.0 + small)
        if side == 0:
            loss[...] += jnp.maximum(value, 0.0) + jnp.log1p(small)
        if diagonal:
            slope = jnp.where(matched, -slope, slope)
        slope = slope.astype(jnp.bfloat16)
        for start in range(0, width, 384):
            columns = slice(start, min(start + 384, width))
            total[side][:, columns] += jnp.dot(slope, here[:, columns], preferred_element_type=jnp.float32)
            if returned:
                back[block(step, CHUNK), columns] = lax.dot_general(
                    slope,
                    own[other:other + rows, columns],
                    (((0,), (0,)), ((), ())),
                    preferred_element_type=jnp.float32,
                ).astype(jnp.bfloat16)

    per = CHUNK // PIECE
    steps = TEXT // CHUNK

    @pl.loop(0, sends)
    def _(piece):
        to_far(piece).wait_recv()

        @pl.loop(piece * steps, (piece + 1) * steps)
        def _(step):
            products(0, far, step, returned=True)
            for part in range(per):
                go_back(step * per + part).start()

        to_near(piece).wait_recv()

        @pl.loop(piece * steps, (piece + 1) * steps)
        def _(step):
            products(0, near, step)

    for side in (0, 1):
        @pl.loop(0, rows // CHUNK)
        def _(step):
            products(side, own, step, diagonal=True)

    loss_out[...] = jnp.sum(loss[...].T, axis=0) / (3.0 * rows)

    @pl.loop(0, rows // FINISH)
    def _(step):
        at = block(step, FINISH)
        finish(image_acc[at, :], image[at, :], image_inv[at, :], scale, image_grad, at)

    @pl.loop(0, sends)
    def _(piece):
        to_near(sends + piece).wait_recv()

        @pl.loop(piece * steps, (piece + 1) * steps)
        def _(step):
            products(1, near, step)

    @pl.loop(0, sends)
    def _(piece):
        to_far(piece).wait_send()
        to_near(piece).wait_send()
        to_near(sends + piece).wait_send()

    @pl.loop(0, pieces)
    def _(piece):
        go_back(piece).wait_recv()
        at = block(piece, PIECE)
        grad = text_acc[at, :] + far[block(piece, PIECE, rows), :].astype(jnp.float32)
        finish(grad, text[at, :], text_inv[at, :], scale, text_grad, at)

    @pl.loop(0, pieces)
    def _(piece):
        go_back(piece).wait_send()


def normalize(emb):
    full = emb.astype(jnp.float32)
    scaled = lax.rsqrt(jnp.sum(full * full, axis=1, keepdims=True) + 1e-06)
    return (full * scaled).astype(jnp.bfloat16), scaled


def finish(grad, emb, inverse, scale, out, at):
    unit = emb.astype(jnp.float32) * inverse
    along = jnp.sum(unit * grad, axis=1, keepdims=True)
    out[at, :] = ((grad - unit * along) * (scale * inverse)).astype(jnp.bfloat16)


def write(loss, image_grad, text_grad, loss_out, image_out, text_out, sem):
    rows = image_grad.shape[0]
    copies = [pltpu.make_async_copy(loss, loss_out, sem.at[0])]
    for side, (source, target) in enumerate(((image_grad, image_out), (text_grad, text_out))):
        for step in range(rows // WRITE):
            at = pl.ds(step * WRITE, WRITE)
            copies.append(pltpu.make_async_copy(source.at[at], target.at[at], sem.at[len(copies)]))
    for copy in copies:
        copy.start()
    for copy in copies:
        copy.wait()


def local(image_emb, text_emb, logit_scale, logit_bias):
    rows, width = image_emb.shape
    n = lax.axis_size("contrast")
    sends = rows // TEXT
    copies = sends + rows // PIECE
    both = pltpu.VMEM((2 * rows, width), jnp.bfloat16)
    dma = pltpu.SemaphoreType.DMA
    shape = jax.ShapeDtypeStruct
    vmem = pl.BlockSpec(memory_space=pltpu.VMEM)
    hbm = pl.BlockSpec(memory_space=pltpu.HBM)
    outs = (shape((rows,), jnp.float32), shape((rows, width), jnp.bfloat16), shape((rows, width), jnp.bfloat16))
    one = pltpu.VMEM((rows, width), jnp.bfloat16)
    wide = pltpu.VMEM((rows, width), jnp.float32)
    column = pltpu.VMEM((rows, 1), jnp.float32)
    handed = pl.pallas_call(
        functools.partial(exchange, n),
        out_shape=outs,
        in_specs=[hbm] * 4,
        out_specs=(vmem,) * 3,
        scratch_shapes=[
            one,
            column,
            wide,
            one,
            column,
            wide,
            both,
            both,
            both,
            one,
            pltpu.VMEM((rows, CHUNK), jnp.float32),
            pltpu.SMEM((1, 1), jnp.float32),
            pltpu.SMEM((1, 1), jnp.float32),
            dma((2,)),
            dma((2 * rows // PREPARE,)),
            dma((copies,)),
            dma((copies,)),
            dma((2 * sends,)),
            dma((2 * sends,)),
        ],
        compiler_params=pltpu.CompilerParams(
            collective_id=0, has_side_effects=True, vmem_limit_bytes=32 * 2**20
        ),
        cost_estimate=pl.CostEstimate(
            flops=22 * rows * rows * width, bytes_accessed=8 * rows * width, transcendentals=15 * rows * rows
        ),
        name="exchange",
    )(
        logit_scale.reshape(1, 1),
        logit_bias.reshape(1, 1),
        pltpu.with_memory_space_constraint(image_emb, pltpu.HBM),
        pltpu.with_memory_space_constraint(text_emb, pltpu.HBM),
    )
    return pl.pallas_call(
        write,
        out_shape=outs,
        in_specs=[vmem] * 3,
        out_specs=(hbm,) * 3,
        scratch_shapes=[dma((2 * rows // WRITE + 1,))],
        compiler_params=pltpu.CompilerParams(vmem_limit_bytes=4 * 2**20),
        cost_estimate=pl.CostEstimate(flops=0, bytes_accessed=8 * rows * width, transcendentals=0),
        name="write",
    )(*handed)


def solution(mesh):
    placed = (P(("dp", "contrast"), None), P(("dp", "contrast"), None), P(), P())
    return jax.shard_map(
        local,
        mesh=mesh,
        in_specs=placed,
        out_specs=(P(("dp", "contrast")), P(("dp", "contrast"), None), P(("dp", "contrast"), None)),
        check_vma=False,
    )
```
